32 devices in a mesh: blk: 4 (over y, x), shard: 8 (over z, core).
Axes of the slice: x: 2, y: 2, z: 4, core: 2. Of those that a mesh axis runs over, the one named last changes fastest.
Arguments:
- table: bfloat16 [65536, 400], P(('blk', 'shard')), may hold values from -3 to 3
- relation: bfloat16 [1345, 400], replicated, may hold values from -3 to 3
- owners: int32 [32768, 2], P(('blk', 'shard')), may hold values from 0 to 7, all different within a row; in each aligned block of 1024 rows (0 to 1023, 1024 to 2047, ...) at most 512 rows name the same one
- rows: int32 [32768, 2], P(('blk', 'shard')), may hold values from 0 to 2047
- rel_ids: int32 [32768], P(('blk', 'shard')), may hold values from 0 to 1344
- span_ids: int32 [32], P(('blk', 'shard')), may hold values from 0 to 1
Outputs:
- entity_grad: float32 [65536, 400], P(('blk', 'shard'))
- relation_grad: float32 [1345, 400], replicated
The draws below stay inside these ranges and needn't reach their ends.
Inputs may be any that keep to these rules, and one draw needn't show every extreme that they name: Among the 1024 edges of one device no owner index is named by more than 512 edge ends; an edge's source and target owners differ; ends address rows of the devices with the same blk index.
All inputs are finite; a program needn't handle non-finite values.
Results may differ from the reference program's by a relative error of at most 0.0016.
Values may be sent and summed in bfloat16 or wider, within the bound.
A program may use at most 128 MiB of HBM per device.

```python
import math
import jax
import jax.numpy as jnp
import numpy as np
from jax import lax

D = 400
REL = 1345
NEG = 1024
E_DEV = 1024
ROWS_OWN = 2048
CAP = 512
EDGES = 32768
ENT = 65536
N_BLK = 4
N_SHARD = 8


def touch_ends(values, key, least, largest):
    extent = values.shape
    index_at = [jax.random.randint(jax.random.fold_in(key, axis), (), 0, extent[axis]) for axis in range(len(extent))]
    values = values.at[tuple(index_at)].set(least)
    longest = extent.index(max(extent))
    index_at[longest] = (index_at[longest] + 1) % extent[longest]
    return values.at[tuple(index_at)].set(largest)


def level_of(stream_key, dims, pieces, least, top_value):
    gain, own = 1.0, jax.random.fold_in(stream_key, 6)
    for axis_at, blocks in pieces:
        steps = jnp.exp(jax.random.uniform(jax.random.fold_in(own, axis_at), (blocks,), jnp.float32, least / len(pieces), top_value / len(pieces)))
        gain = gain * jnp.repeat(steps, dims[axis_at] // blocks).reshape([-1 if axis == axis_at else 1 for axis in range(len(dims))])
    return gain


def rank_bounds(count, skew):
    portions = [(1 << 20) // math.isqrt(rank ** skew) + 1 for rank in range(1, count + 1)]
    deviation = 1 + sum(portions) // (1 << 30)
    return np.cumsum(np.array([max(1, weight // deviation) for weight in portions]))


def ranked_ids(stream_key, extent, amount, skew):
    table = rank_bounds(amount, skew)
    pick = jax.random.randint(jax.random.fold_in(stream_key, 1), extent, 0, int(table[amount - 1]))
    grade = jnp.searchsorted(jnp.asarray(table, jnp.int32), pick, side="right")
    return jax.random.permutation(jax.random.fold_in(stream_key, 2), amount)[grade].astype(jnp.int32)


def deal_out(key, own, number, rows, number_of, top, most, slope):
    ranking = jax.random.permutation(key, number_of)
    heavy_load, common = load_shares(number_of, rows * top, most, slope, True), load_shares(number_of, rows * top, most, slope, False)
    places = jnp.arange(number_of)

    def named(tallies, rotation):
        used = int((tallies > 0).sum())
        fixed = max(1, used // 4)
        passed = fixed + (places - fixed + rotation * (used - fixed)) % max(1, number_of - fixed)
        return jnp.zeros((number_of,), jnp.int32).at[ranking[jnp.where(places < fixed, places, passed)]].set(jnp.asarray(tallies, jnp.int32))

    tallies = jnp.where(number % 4 == 0, named(heavy_load, number // 4), named(common, number - number // 4 - 1))
    mixed = jax.random.permutation(jax.random.fold_in(own, 3), number_of)
    source_of, taker = mixed[0:number_of // 2 * 2:2], mixed[1:number_of // 2 * 2:2]
    room = jnp.minimum(tallies[source_of] - 1, most - tallies[taker]) // 2
    room = jnp.where((source_of == ranking[0]) | (taker == ranking[0]) | (tallies[taker] == 0), 0, jnp.maximum(room, 0))
    passed = jax.random.randint(jax.random.fold_in(own, 4), (number_of // 2,), 0, 1 << 20) % (room + 1)
    tallies = tallies.at[source_of].add(-passed).at[taker].add(passed)
    labels = jnp.searchsorted(jnp.cumsum(tallies), jnp.arange(rows * top), side="right").astype(jnp.int32)
    listing = labels.reshape(top, rows).T
    listing = listing[jax.random.permutation(jax.random.fold_in(own, 1), rows)]
    rotation = jax.random.randint(jax.random.fold_in(own, 2), (rows, 1), 0, top)
    return jnp.take_along_axis(listing, (jnp.arange(top)[None, :] + rotation) % top, axis=1)


def load_shares(amount, total, bound, slope, full):
    loads = [(1 << 20) // math.isqrt(standing ** slope) + 1 for standing in range(1, amount + 1)]
    largest = bound if full else min(bound, max(-(-total // amount), total * loads[0] // sum(loads)))
    least = 1 if total - largest >= amount - 1 else 0
    holding, surplus = [largest] + [least] * (amount - 1), total - largest - least * (amount - 1)
    while surplus > 0:
        candidates = [i for i in range(1, amount) if holding[i] < largest] or [i for i in range(1, amount) if holding[i] < bound]
        whole, left = sum([loads[i] for i in candidates]), surplus
        for i in candidates:
            addition = min(bound - holding[i], max(1, left * loads[i] // whole), surplus)
            holding[i] = holding[i] + addition
            surplus = surplus - addition
    return np.array(holding)


def bell_draw(rng, dims, deviation, reach, cuts=(), kind=jnp.bfloat16):
    array = jax.random.normal(rng, dims, jnp.float32) * deviation
    if len(cuts) > 0:
        array = level_of(rng, dims, cuts, -0.22, 0.18) * array
    return jnp.clip(array, min=-reach, max=reach).astype(kind)


def setup_inputs(seed: int = 0) -> dict:
    key_of = jax.random.split(jax.random.key(seed), 7)
    table = bell_draw(key_of[0], (ENT, D), 0.5, 3.0, ((0, 32),))
    relation = bell_draw(key_of[1], (REL, D), 0.5, 3.0)
    owners_keys = jax.random.split(jax.random.fold_in(key_of[2], 1), EDGES // E_DEV)
    owners_turns = jax.random.permutation(jax.random.fold_in(key_of[2], 3), EDGES // E_DEV)
    owners = jax.vmap(lambda own, number: deal_out(jax.random.fold_in(key_of[2], 2), own, number, E_DEV, N_SHARD, 2, CAP, 2))(owners_keys, owners_turns).reshape((EDGES, 2))
    rows = touch_ends(ranked_ids(key_of[3], (EDGES, 2), ROWS_OWN, 2), jax.random.fold_in(key_of[3], 3), 0, ROWS_OWN - 1).astype(jnp.int32)
    rel_ids = touch_ends(ranked_ids(key_of[4], (EDGES,), REL, 2), jax.random.fold_in(key_of[4], 3), 0, REL - 1).astype(jnp.int32)
    span_ids = touch_ends(jax.random.randint(key_of[5], (N_BLK * N_SHARD,), 0, ROWS_OWN // NEG), jax.random.fold_in(key_of[5], 1), 0, (ROWS_OWN // NEG) - 1).astype(jnp.int32)
    return dict(table=table, relation=relation, owners=owners, rows=rows, rel_ids=rel_ids, span_ids=span_ids)


def edge_terms(source, target, rel_rows, spans, weight):
    half = source.shape[1] // 2
    s_re, s_im = source[:, :half], source[:, half:]
    r_re, r_im = rel_rows[:, :half], rel_rows[:, half:]
    query = jnp.concatenate([s_re * r_re - s_im * r_im, s_re * r_im + s_im * r_re], axis=1)
    pos_score = jnp.sum(query * target, axis=1)
    pos_grad = jax.nn.sigmoid(pos_score) - 1.0
    query_bf = lax.optimization_barrier(query.astype(jnp.bfloat16)).astype(jnp.float32)
    neg_score = jnp.einsum("ed,cnd->cen", query_bf, spans)
    neg_grad = lax.optimization_barrier((weight * jax.nn.sigmoid(neg_score)).astype(jnp.bfloat16)).astype(jnp.float32)
    query_grad = pos_grad[:, None] * target + jnp.einsum("cen,cnd->ed", neg_grad, spans)
    q_re, q_im = query_grad[:, :half], query_grad[:, half:]
    source_grad = jnp.concatenate([q_re * r_re + q_im * r_im, q_im * r_re - q_re * r_im], axis=1)
    rel_term = jnp.concatenate([q_re * s_re + q_im * s_im, q_im * s_re - q_re * s_im], axis=1)
    target_grad = pos_grad[:, None] * query
    span_term = jnp.einsum("cen,ed->cnd", neg_grad, query_bf)
    return source_grad, target_grad, rel_term, span_term


def reference(table, relation, owners, rows, rel_ids, span_ids):
    devices = N_BLK * N_SHARD
    edge_index = jnp.arange(EDGES, dtype=jnp.int32)
    blk_of = (edge_index // E_DEV) // N_SHARD
    ids = ((blk_of[:, None] * N_SHARD + owners) * ROWS_OWN + rows).astype(jnp.int32)
    starts = (jnp.arange(devices, dtype=jnp.int32) * ROWS_OWN + span_ids * NEG).astype(jnp.int32)
    weight = 1.0 / (float(N_BLK * NEG) ** 0.5)
    peer_table = (jnp.arange(N_BLK, dtype=jnp.int32)[None, :] * N_SHARD
                  + (jnp.arange(devices, dtype=jnp.int32) % N_SHARD)[:, None]).astype(jnp.int32)

    def one_device(device):
        first = (device * E_DEV).astype(jnp.int32)
        own_ids = lax.dynamic_slice(ids, (first, jnp.int32(0)), (E_DEV, 2))
        source = table[own_ids[:, 0]].astype(jnp.float32)
        target = table[own_ids[:, 1]].astype(jnp.float32)
        rel_rows = relation[lax.dynamic_slice(rel_ids, (first,), (E_DEV,))].astype(jnp.float32)
        peer_starts = starts[peer_table[device]]
        spans = jax.vmap(lambda begin: lax.dynamic_slice_in_dim(table, begin, NEG, 0))(peer_starts).astype(jnp.float32)
        return edge_terms(source, target, rel_rows, spans, weight)

    source_grad, target_grad, rel_term, span_term = lax.map(one_device, jnp.arange(devices, dtype=jnp.int32))
    entity_grad = jnp.zeros((ENT, D), jnp.float32)
    entity_grad = entity_grad.at[ids[:, 0]].add(source_grad.reshape(EDGES, D))
    entity_grad = entity_grad.at[ids[:, 1]].add(target_grad.reshape(EDGES, D))
    span_rows = (starts[peer_table][:, :, None] + jnp.arange(NEG, dtype=jnp.int32)[None, None, :]).astype(jnp.int32)
    entity_grad = entity_grad.at[span_rows.reshape(-1)].add(span_term.reshape(-1, D))
    relation_grad = jnp.zeros((REL, D), jnp.float32).at[rel_ids].add(rel_term.reshape(EDGES, D))
    return entity_grad, relation_grad
```

```python
import functools
import math

import jax
import jax.numpy as jnp
from jax import lax
from jax.experimental import pallas as pl
from jax.experimental.pallas import tpu as pltpu
from jax.sharding import PartitionSpec as P

NEG = 1024
F32 = jnp.float32
BF = jnp.bfloat16
MESH = pl.DeviceIdType.MESH
NN = (((1,), (0,)), ((), ()))
NT = (((1,), (1,)), ((), ()))
TN = (((0,), (0,)), ((), ()))


def dot(a, b, dims):
    return lax.dot_general(a, b, dims, preferred_element_type=F32)


def onehot(count, first, ids):
    at = lax.broadcasted_iota(jnp.int32, (count, ids.shape[1]), 0) + first
    return jnp.where(at == ids, 1.0, 0.0).astype(BF)


def kernel(
    n, nb, cap, piece,
    table, relation, slots, wanted, rel_ids, span_id,
    entity, relation_out,
    req_out, req_in, row_out, row_in, grad_in,
    spans, back_out, back_in, own_back,
    rel_pad, rel_rows, query_s, query_bf, query_grad, end_grads, rel_lo,
    r1_out, r1_in, r2_out, r2_in, r3, r4_in,
    req_ss, req_rs, row_ss, row_rs, grad_ss, grad_rs,
    span_ss, span_rs, back_ss, back_rs, r1_ss, r1_rs, r2_ss, r2_rs, r3_ss, r3_rs, r4_ss, r4_rs,
):
    width, own_rows = table.shape
    half = width // 2
    edges = rel_ids.shape[1]
    types = relation.shape[1]
    part = r3.shape[1]
    negatives = spans.shape[2]
    weight = 1.0 / math.sqrt(nb * negatives)
    ends, rel_hi, grad_out = entity, query_bf, row_out
    chunk = 512
    me, mb = lax.axis_index("shard"), lax.axis_index("blk")

    barrier = pltpu.get_barrier_semaphore()

    def greet(i, _):
        pl.semaphore_signal(
            barrier, inc=1, device_id={"shard": lax.rem(me + i, n)}, device_id_type=MESH
        )
        return 0

    lax.fori_loop(1, n, greet, 0)
    for i in range(1, nb):
        pl.semaphore_signal(
            barrier, inc=1, device_id={"blk": lax.rem(mb + i, nb)}, device_id_type=MESH
        )
    pl.semaphore_wait(barrier, n + nb - 2)

    def to_shard(src, dst, ss, rs, to, frm):
        return pltpu.make_async_remote_copy(
            src_ref=src, dst_ref=dst, send_sem=ss.at[to], recv_sem=rs.at[frm],
            device_id={"shard": to}, device_id_type=MESH,
        )

    def to_blk(src, dst, ss, rs, to, frm):
        return pltpu.make_async_remote_copy(
            src_ref=src, dst_ref=dst, send_sem=ss.at[to], recv_sem=rs.at[frm],
            device_id={"blk": to}, device_id_type=MESH,
        )

    def peers(body):
        def step(i, _):
            body(lax.rem(me + i, n))
            return 0

        lax.fori_loop(1, n, step, 0)

    def blk_peers(body):
        for i in range(1, nb):
            body(lax.rem(mb + i, nb))

    sid = span_id[...]
    mine = table[:, 0:negatives]
    for h in range(1, own_rows // negatives):
        mine = jnp.where(sid == h, table[:, h * negatives:(h + 1) * negatives], mine)
    spans[mb] = mine

    def send_span(c):
        to_blk(spans.at[mb], spans.at[mb], span_ss, span_rs, c, mb).start()

    blk_peers(send_span)

    def ask(q):
        acc = jnp.zeros((wanted.shape[0], cap), F32)
        for e in range(0, 2 * edges, chunk):
            pick = onehot(cap, q * cap, slots[:, e:e + chunk])
            acc = acc + dot(wanted[:, e:e + chunk], pick, NT)
        return acc[0:8]

    def send_ask(q):
        req_out[q] = ask(q)
        to_shard(req_out.at[q], req_in.at[me], req_ss, req_rs, q, me).start()

    peers(send_ask)
    req_in[me] = ask(me)

    def asked(q):
        both = req_in[q]
        return (both[0:1] * 256.0 + both[1:2]).astype(jnp.int32)

    def look_up(q):
        ids = asked(q)
        acc = jnp.zeros((width, cap), F32)
        for r in range(0, own_rows, chunk):
            acc = acc + dot(table[:, r:r + chunk], onehot(chunk, r, ids), NN)
        return acc.astype(BF)

    def send_rows(q):
        to_shard(req_out.at[q], req_in.at[q], req_ss, req_rs, q, q).wait_recv()
        row_out[q] = look_up(q)
        to_shard(row_out.at[q], row_in.at[me], row_ss, row_rs, q, me).start()

    peers(send_rows)
    row_in[me] = look_up(me)

    rel_pad[...] = jnp.zeros(rel_pad.shape, BF)
    rel_pad[:, 0:types] = relation[...]
    for e in range(0, edges, chunk):
        acc = jnp.zeros((width, chunk), F32)
        for r in range(0, rel_pad.shape[1], part):
            acc = acc + dot(rel_pad[:, r:r + part], onehot(part, r, rel_ids[:, e:e + chunk]), NN)
        rel_rows[:, e:e + chunk] = acc

    def place(q, first):
        rows = row_in[q]
        for e in range(0, 2 * edges, chunk):
            add = dot(rows, onehot(cap, q * cap, slots[:, e:e + chunk]), NN)
            if first:
                ends[:, e:e + chunk] = add
            else:
                ends[:, e:e + chunk] += add

    place(me, True)

    def take_rows(q):
        to_shard(row_out.at[q], row_in.at[q], row_ss, row_rs, q, q).wait_recv()
        place(q, False)

    peers(take_rows)

    block = 128

    def query_step(j, _):
        at = pl.ds(pl.multiple_of(j * block, block), block)
        at_target = pl.ds(pl.multiple_of(edges + j * block, block), block)
        s_re, s_im = ends[0:half, at], ends[half:width, at]
        r_re, r_im = rel_rows[0:half, at], rel_rows[half:width, at]
        t_re, t_im = ends[0:half, at_target], ends[half:width, at_target]
        a = s_re * r_re - s_im * r_im
        b = s_re * r_im + s_im * r_re
        score = jnp.sum(a * t_re, axis=0, keepdims=True) + jnp.sum(b * t_im, axis=0, keepdims=True)
        pos = jax.nn.sigmoid(score) - 1.0
        query_s[0:half, at] = a
        query_s[half:width, at] = b
        query_grad[0:half, at] = pos * t_re
        query_grad[half:width, at] = pos * t_im
        end_grads[:, at_target] = (pos * query_s[:, at]).astype(BF)
        query_bf[:, at] = query_s[:, at].astype(BF)
        return 0

    lax.fori_loop(0, edges // block, query_step, 0)

    tile = 256

    def visit(c, own):
        def step(j, _):
            at = pl.ds(pl.multiple_of(j * tile, tile), tile)
            sp = spans[c, :, at]
            score = dot(sp, query_bf[...], TN)
            g = (weight * jax.nn.sigmoid(score)).astype(BF)
            query_grad[...] += dot(sp, g, NN)
            term = dot(query_bf[...], g, NT)
            if own:
                own_back[:, at] = term
            else:
                back_out[c, :, at] = term.astype(BF)
            return 0

        lax.fori_loop(0, negatives // tile, step, 0)

    def peer_visit(i, _):
        c = lax.rem(mb + i, nb)
        to_blk(spans.at[c], spans.at[c], span_ss, span_rs, c, c).wait_recv()
        visit(c, False)
        to_blk(back_out.at[c], back_in.at[mb], back_ss, back_rs, c, mb).start()
        return 0

    lax.fori_loop(1, nb, peer_visit, 0)
    visit(mb, True)

    def grad_step(j, _):
        at = pl.ds(pl.multiple_of(j * block, block), block)
        s_re, s_im = ends[0:half, at], ends[half:width, at]
        r_re, r_im = rel_rows[0:half, at], rel_rows[half:width, at]
        q_re, q_im = query_grad[0:half, at], query_grad[half:width, at]
        query_s[0:half, at] = q_re * r_re + q_im * r_im
        query_s[half:width, at] = q_im * r_re - q_re * r_im
        end_grads[:, at] = query_s[:, at].astype(BF)
        rel_rows[0:half, at] = q_re * s_re + q_im * s_im
        rel_rows[half:width, at] = q_im * s_re - q_re * s_im
        term = rel_rows[:, at]
        hi = term.astype(BF)
        rel_hi[:, at] = hi
        rel_lo[:, at] = (term - hi.astype(F32)).astype(BF)
        return 0

    lax.fori_loop(0, edges // block, grad_step, 0)

    def rel_sum(c):
        acc = jnp.zeros((width, part), F32)
        for e in range(0, edges, chunk):
            pick = onehot(part, c * part, rel_ids[:, e:e + chunk])
            acc = acc + dot(rel_hi[:, e:e + chunk], pick, NT)
            acc = acc + dot(rel_lo[:, e:e + chunk], pick, NT)
        return acc

    def send_rel(i, _):
        c = lax.rem(mb + i, nb)
        r1_out[c] = rel_sum(c)
        to_blk(r1_out.at[c], r1_in.at[mb], r1_ss, r1_rs, c, mb).start()
        return 0

    lax.fori_loop(1, nb, send_rel, 0)

    def collect(q):
        acc = jnp.zeros((width, cap), F32)
        for e in range(0, 2 * edges, chunk):
            pick = onehot(cap, q * cap, slots[:, e:e + chunk])
            acc = acc + dot(end_grads[:, e:e + chunk], pick, NT)
        return acc.astype(BF)

    def send_grads(q):
        to_shard(row_out.at[q], row_in.at[me], row_ss, row_rs, q, me).wait_send()
        grad_out[q] = collect(q)
        to_shard(grad_out.at[q], grad_in.at[me], grad_ss, grad_rs, q, me).start()

    peers(send_grads)
    grad_in[me] = collect(me)
    r1_in[mb] = rel_sum(mb)

    def settle(q, first):
        ids = asked(q)
        got = grad_in[q]
        for r in range(0, own_rows, chunk):
            add = dot(got, onehot(chunk, r, ids), NT)
            if first:
                entity[:, r:r + chunk] = add
            else:
                entity[:, r:r + chunk] += add

    def take_r1(c):
        to_blk(r1_out.at[c], r1_in.at[c], r1_ss, r1_rs, c, c).wait_recv()

    blk_peers(take_r1)
    total = r1_in[0]
    for c in range(1, nb):
        total = total + r1_in[c]
    r2_out[...] = jnp.zeros(r2_out.shape, BF)
    r2_out[0:width] = total.astype(BF)

    def piece_at(q):
        return pl.ds(pl.multiple_of(q * piece, piece), piece)

    def send_r2(q):
        to_shard(r2_out.at[piece_at(q)], r2_in.at[me], r2_ss, r2_rs, q, me).start()

    peers(send_r2)
    r2_in[me] = r2_out[piece_at(me)]
    settle(me, True)

    def take_r2(q):
        to_shard(r2_out.at[piece_at(q)], r2_in.at[q], r2_ss, r2_rs, q, q).wait_recv()

    peers(take_r2)

    def add_r2(q, acc):
        return acc + r2_in[q].astype(F32)

    r3[piece_at(me)] = lax.fori_loop(0, n, add_r2, jnp.zeros((piece, part), F32))

    def send_r3(q):
        to_shard(r3.at[piece_at(me)], r3.at[piece_at(me)], r3_ss, r3_rs, q, me).start()

    peers(send_r3)

    def take_r3(q):
        to_shard(r3.at[piece_at(q)], r3.at[piece_at(q)], r3_ss, r3_rs, q, q).wait_recv()

    peers(take_r3)
    whole = r3.at[pl.ds(0, width)]

    def send_r4(c):
        to_blk(whole, r4_in.at[mb], r4_ss, r4_rs, c, mb).start()

    blk_peers(send_r4)
    r4_in[mb] = r3[0:width]

    def take_grads(q):
        to_shard(grad_out.at[q], grad_in.at[q], grad_ss, grad_rs, q, q).wait_recv()
        settle(q, False)

    peers(take_grads)

    def take_back(c):
        to_blk(back_out.at[c], back_in.at[c], back_ss, back_rs, c, c).wait_recv()
        own_back[...] += back_in[c].astype(F32)

    blk_peers(take_back)
    for h in range(own_rows // negatives):
        entity[:, h * negatives:(h + 1) * negatives] += jnp.where(sid == h, own_back[...], 0.0)

    def take_r4(c):
        to_blk(whole, r4_in.at[c], r4_ss, r4_rs, c, c).wait_recv()

    blk_peers(take_r4)
    for c in range(nb):
        wide = min(part, types - c * part)
        if wide > 0:
            relation_out[:, c * part:c * part + wide] = r4_in[c][:, 0:wide]

    def finish(q):
        to_shard(req_out.at[q], req_in.at[me], req_ss, req_rs, q, me).wait_send()
        to_shard(grad_out.at[q], grad_in.at[me], grad_ss, grad_rs, q, me).wait_send()
        to_shard(r2_out.at[piece_at(q)], r2_in.at[me], r2_ss, r2_rs, q, me).wait_send()
        to_shard(r3.at[piece_at(me)], r3.at[piece_at(me)], r3_ss, r3_rs, q, me).wait_send()

    peers(finish)

    def finish_blk(c):
        to_blk(spans.at[mb], spans.at[mb], span_ss, span_rs, c, mb).wait_send()
        to_blk(back_out.at[c], back_in.at[mb], back_ss, back_rs, c, mb).wait_send()
        to_blk(r1_out.at[c], r1_in.at[mb], r1_ss, r1_rs, c, mb).wait_send()
        to_blk(whole, r4_in.at[mb], r4_ss, r4_rs, c, mb).wait_send()

    blk_peers(finish_blk)


def round_up(a, b):
    return -(-a // b) * b


def shards(table, relation, owners, rows, rel_ids, span_ids):
    n = lax.axis_size("shard")
    nb = lax.axis_size("blk")
    edges = owners.shape[0]
    own_rows, width = table.shape
    types = relation.shape[0]
    cap = 4 * edges // n
    part = round_up(-(-types // nb), 128)
    piece = round_up(-(-width // n), 16)
    flat_owner = owners.T.reshape(-1)
    flat_row = rows.T.reshape(-1)
    hot = (flat_owner[None, :] == jnp.arange(n, dtype=jnp.int32)[:, None]).astype(jnp.int32)
    ranking = jnp.sum(jnp.cumsum(hot, axis=1) * hot, axis=0) - 1
    slots = (flat_owner * cap + ranking).reshape(1, 2 * edges)
    wanted = jnp.concatenate(
        [(flat_row // 256)[None], (flat_row % 256)[None], jnp.zeros((14, 2 * edges), jnp.int32)]
    ).astype(BF)

    vm = pltpu.VMEM
    dma = pltpu.SemaphoreType.DMA
    scratch = [
        vm((n, 8, cap), F32), vm((n, 8, cap), F32),
        vm((n, width, cap), BF), vm((n, width, cap), BF), vm((n, width, cap), BF),
        vm((nb, width, NEG), BF), vm((nb, width, NEG), BF), vm((nb, width, NEG), BF),
        vm((width, NEG), F32),
        vm((width, nb * part), BF), vm((width, edges), F32),
        vm((width, edges), F32), vm((width, edges), BF), vm((width, edges), F32),
        vm((width, 2 * edges), BF), vm((width, edges), BF),
        vm((nb, width, part), F32), vm((nb, width, part), F32),
        vm((n * piece, part), BF), vm((n, piece, part), BF), vm((n * piece, part), F32),
        vm((nb, width, part), F32),
    ]
    scratch += [dma((n,))] * 6 + [dma((nb,))] * 6 + [dma((n,))] * 4 + [dma((nb,))] * 2
    spec = pl.BlockSpec(memory_space=pltpu.VMEM)
    entity, rel_grad = pl.pallas_call(
        functools.partial(kernel, n, nb, cap, piece),
        out_shape=(
            jax.ShapeDtypeStruct((width, own_rows), F32),
            jax.ShapeDtypeStruct((width, types), F32),
        ),
        in_specs=[spec] * 6,
        out_specs=(spec, spec),
        scratch_shapes=scratch,
        compiler_params=pltpu.CompilerParams(
            collective_id=0, has_side_effects=True, vmem_limit_bytes=60 * 1024 * 1024
        ),
    )(table.T, relation.T, slots, wanted, rel_ids.reshape(1, edges), span_ids.reshape(1, 1))
    return (entity.T, rel_grad.T)


def solution(mesh):
    in_specs = (
        P(("blk", "shard"), None),
        P(),
        P(("blk", "shard"), None),
        P(("blk", "shard"), None),
        P(("blk", "shard")),
        P(("blk", "shard")),
    )
    out_specs = (P(("blk", "shard"), None), P())
    return jax.shard_map(shards, mesh=mesh, in_specs=in_specs, out_specs=out_specs, check_vma=False)
```

```python
import functools
import math

import jax
import jax.numpy as jnp
from jax import lax
from jax.experimental import pallas as pl
from jax.experimental.pallas import tpu as pltpu
from jax.sharding import PartitionSpec as P

NEG = 1024
F32 = jnp.float32
BF = jnp.bfloat16
MESH = pl.DeviceIdType.MESH
NN = (((1,), (0,)), ((), ()))
NT = (((1,), (1,)), ((), ()))
TN = (((0,), (0,)), ((), ()))


def dot(a, b, dims):
    return lax.dot_general(a, b, dims, preferred_element_type=F32)


def onehot(count, first, ids):
    at = lax.broadcasted_iota(jnp.int32, (count, ids.shape[1]), 0) + first
    return jnp.where(at == ids, 1.0, 0.0).astype(BF)


def kernel(
    n, nb, cap, piece,
    table, relation, slots, wanted, rel_ids, span_id,
    entity, relation_out,
    req_out, req_in, row_out, row_in, grad_in,
    spans, back_out, back_in, own_back,
    rel_pad, rel_rows, query_s, query_bf, query_grad, end_grads, rel_lo,
    r1_out, r1_in, r2_out, r2_in, r3, r4_in,
    req_ss, req_rs, row_ss, row_rs, grad_ss, grad_rs,
    span_ss, span_rs, back_ss, back_rs, r1_ss, r1_rs, r2_ss, r2_rs, r3_ss, r3_rs, r4_ss, r4_rs,
):
    width, own_rows = table.shape
    half = width // 2
    edges = rel_ids.shape[1]
    types = relation.shape[1]
    part = r3.shape[1]
    negatives = spans.shape[2]
    weight = 1.0 / math.sqrt(nb * negatives)
    ends, rel_hi, grad_out = entity, query_bf, row_out
    chunk = 512
    me, mb = lax.axis_index("shard"), lax.axis_index("blk")

    barrier = pltpu.get_barrier_semaphore()

    def greet(i, _):
        pl.semaphore_signal(
            barrier, inc=1, device_id={"shard": lax.rem(me + i, n)}, device_id_type=MESH
        )
        return 0

    lax.fori_loop(1, n, greet, 0)
    for i in range(1, nb):
        pl.semaphore_signal(
            barrier, inc=1, device_id={"blk": lax.rem(mb + i, nb)}, device_id_type=MESH
        )
    pl.semaphore_wait(barrier, n + nb - 2)

    def to_shard(src, dst, ss, rs, to, frm):
        return pltpu.make_async_remote_copy(
            src_ref=src, dst_ref=dst, send_sem=ss.at[to], recv_sem=rs.at[frm],
            device_id={"shard": to}, device_id_type=MESH,
        )

    def to_blk(src, dst, ss, rs, to, frm):
        return pltpu.make_async_remote_copy(
            src_ref=src, dst_ref=dst, send_sem=ss.at[to], recv_sem=rs.at[frm],
            device_id={"blk": to}, device_id_type=MESH,
        )

    def peers(body, first=1, last=n):
        def step(i, _):
            body(lax.rem(me + i, n))
            return 0

        lax.fori_loop(first, last, step, 0)

    def senders(body, first=1, last=n):
        def step(i, _):
            body(lax.rem(me + n - i, n))
            return 0

        lax.fori_loop(first, last, step, 0)

    def blk_peers(body):
        for i in range(1, nb):
            body(lax.rem(mb + i, nb))

    sid = span_id[...]
    mine = table[:, 0:negatives]
    for h in range(1, own_rows // negatives):
        mine = jnp.where(sid == h, table[:, h * negatives:(h + 1) * negatives], mine)
    spans[mb] = mine

    def send_span(c):
        to_blk(spans.at[mb], spans.at[mb], span_ss, span_rs, c, mb).start()

    blk_peers(send_span)

    def ask(q):
        acc = jnp.zeros((wanted.shape[0], cap), F32)
        for e in range(0, 2 * edges, chunk):
            pick = onehot(cap, q * cap, slots[:, e:e + chunk])
            acc = acc + dot(wanted[:, e:e + chunk], pick, NT)
        return acc[0:8]

    def send_ask(q):
        req_out[q] = ask(q)
        to_shard(req_out.at[q], req_in.at[me], req_ss, req_rs, q, me).start()

    peers(send_ask)
    req_in[me] = ask(me)

    def asked(q):
        both = req_in[q]
        return (both[0:1] * 256.0 + both[1:2]).astype(jnp.int32)

    def look_up(q):
        ids = asked(q)
        acc = jnp.zeros((width, cap), F32)
        for r in range(0, own_rows, chunk):
            acc = acc + dot(table[:, r:r + chunk], onehot(chunk, r, ids), NN)
        return acc.astype(BF)

    def send_rows(q):
        to_shard(req_out.at[q], req_in.at[q], req_ss, req_rs, q, q).wait_recv()
        row_out[q] = look_up(q)
        to_shard(row_out.at[q], row_in.at[me], row_ss, row_rs, q, me).start()

    peers(send_rows)
    row_in[me] = look_up(me)

    rel_pad[...] = jnp.zeros(rel_pad.shape, BF)
    rel_pad[:, 0:types] = relation[...]
    for e in range(0, edges, chunk):
        acc = jnp.zeros((width, chunk), F32)
        for r in range(0, rel_pad.shape[1], part):
            acc = acc + dot(rel_pad[:, r:r + part], onehot(part, r, rel_ids[:, e:e + chunk]), NN)
        rel_rows[:, e:e + chunk] = acc

    def place(q, first):
        rows = row_in[q]
        for e in range(0, 2 * edges, chunk):
            add = dot(rows, onehot(cap, q * cap, slots[:, e:e + chunk]), NN)
            if first:
                ends[:, e:e + chunk] = add
            else:
                ends[:, e:e + chunk] += add

    place(me, True)

    def take_rows(q):
        to_shard(row_out.at[q], row_in.at[q], row_ss, row_rs, q, q).wait_recv()
        place(q, False)

    senders(take_rows)

    block = 128

    def query_step(j, _):
        at = pl.ds(pl.multiple_of(j * block, block), block)
        at_target = pl.ds(pl.multiple_of(edges + j * block, block), block)
        s_re, s_im = ends[0:half, at], ends[half:width, at]
        r_re, r_im = rel_rows[0:half, at], rel_rows[half:width, at]
        t_re, t_im = ends[0:half, at_target], ends[half:width, at_target]
        a = s_re * r_re - s_im * r_im
        b = s_re * r_im + s_im * r_re
        score = jnp.sum(a * t_re, axis=0, keepdims=True) + jnp.sum(b * t_im, axis=0, keepdims=True)
        pos = jax.nn.sigmoid(score) - 1.0
        query_s[0:half, at] = a
        query_s[half:width, at] = b
        query_grad[0:half, at] = pos * t_re
        query_grad[half:width, at] = pos * t_im
        end_grads[:, at_target] = (pos * query_s[:, at]).astype(BF)
        query_bf[:, at] = query_s[:, at].astype(BF)
        return 0

    lax.fori_loop(0, edges // block, query_step, 0)

    tile = 256

    def visit(c, own):
        def step(j, _):
            at = pl.ds(pl.multiple_of(j * tile, tile), tile)
            sp = spans[c, :, at]
            score = dot(sp, query_bf[...], TN)
            g = (weight * jax.nn.sigmoid(score)).astype(BF)
            query_grad[...] += dot(sp, g, NN)
            term = dot(query_bf[...], g, NT)
            if own:
                own_back[:, at] = term
            else:
                back_out[c, :, at] = term.astype(BF)
            return 0

        lax.fori_loop(0, negatives // tile, step, 0)

    def peer_visit(i, _):
        c = lax.rem(mb + nb - i, nb)
        to_blk(spans.at[c], spans.at[c], span_ss, span_rs, c, c).wait_recv()
        visit(c, False)
        return 0

    visit(mb, True)
    lax.fori_loop(1, nb, peer_visit, 0)

    def grad_step(j, _):
        at = pl.ds(pl.multiple_of(j * block, block), block)
        s_re, s_im = ends[0:half, at], ends[half:width, at]
        r_re, r_im = rel_rows[0:half, at], rel_rows[half:width, at]
        q_re, q_im = query_grad[0:half, at], query_grad[half:width, at]
        query_s[0:half, at] = q_re * r_re + q_im * r_im
        query_s[half:width, at] = q_im * r_re - q_re * r_im
        end_grads[:, at] = query_s[:, at].astype(BF)
        rel_rows[0:half, at] = q_re * s_re + q_im * s_im
        rel_rows[half:width, at] = q_im * s_re - q_re * s_im
        term = rel_rows[:, at]
        hi = term.astype(BF)
        rel_hi[:, at] = hi
        rel_lo[:, at] = (term - hi.astype(F32)).astype(BF)
        return 0

    lax.fori_loop(0, edges // block, grad_step, 0)

    def rel_sum(c):
        acc = jnp.zeros((width, part), F32)
        for e in range(0, edges, chunk):
            pick = onehot(part, c * part, rel_ids[:, e:e + chunk])
            acc = acc + dot(rel_hi[:, e:e + chunk], pick, NT)
            acc = acc + dot(rel_lo[:, e:e + chunk], pick, NT)
        return acc

    def send_rel(i, _):
        c = lax.rem(mb + i, nb)
        r1_out[c] = rel_sum(c)
        to_blk(r1_out.at[c], r1_in.at[mb], r1_ss, r1_rs, c, mb).start()
        return 0

    lax.fori_loop(1, nb, send_rel, 0)

    def send_back(c):
        to_blk(back_out.at[c], back_in.at[mb], back_ss, back_rs, c, mb).start()

    blk_peers(send_back)

    def collect(q):
        acc = jnp.zeros((width, cap), F32)
        for e in range(0, 2 * edges, chunk):
            pick = onehot(cap, q * cap, slots[:, e:e + chunk])
            acc = acc + dot(end_grads[:, e:e + chunk], pick, NT)
        return acc.astype(BF)

    def send_grads(q):
        to_shard(row_out.at[q], row_in.at[me], row_ss, row_rs, q, me).wait_send()
        grad_out[q] = collect(q)
        to_shard(grad_out.at[q], grad_in.at[me], grad_ss, grad_rs, q, me).start()

    lot_1 = 1 + n // 2
    lot_2 = n - max(1, n // 8)
    peers(send_grads, 1, lot_1)
    grad_in[me] = collect(me)
    r1_in[mb] = rel_sum(mb)

    def settle(q, first):
        ids = asked(q)
        got = grad_in[q]
        for r in range(0, own_rows, chunk):
            add = dot(got, onehot(chunk, r, ids), NT)
            if first:
                entity[:, r:r + chunk] = add
            else:
                entity[:, r:r + chunk] += add

    def take_r1(c):
        to_blk(r1_out.at[c], r1_in.at[c], r1_ss, r1_rs, c, c).wait_recv()

    blk_peers(take_r1)
    total = r1_in[0]
    for c in range(1, nb):
        total = total + r1_in[c]
    r2_out[...] = jnp.zeros(r2_out.shape, BF)
    r2_out[0:width] = total.astype(BF)

    def piece_at(q):
        return pl.ds(pl.multiple_of(q * piece, piece), piece)

    def send_r2(q):
        to_shard(r2_out.at[piece_at(q)], r2_in.at[me], r2_ss, r2_rs, q, me).start()

    peers(send_r2)
    peers(send_grads, lot_1, lot_2)
    r2_in[me] = r2_out[piece_at(me)]
    settle(me, True)

    def take_r2(q):
        to_shard(r2_out.at[piece_at(q)], r2_in.at[q], r2_ss, r2_rs, q, q).wait_recv()

    peers(take_r2)

    def add_r2(q, acc):
        return acc + r2_in[q].astype(F32)

    r3[piece_at(me)] = lax.fori_loop(0, n, add_r2, jnp.zeros((piece, part), F32))

    def send_r3(q):
        to_shard(r3.at[piece_at(me)], r3.at[piece_at(me)], r3_ss, r3_rs, q, me).start()

    peers(send_r3)
    peers(send_grads, lot_2, n)

    def take_grads(q):
        to_shard(grad_out.at[q], grad_in.at[q], grad_ss, grad_rs, q, q).wait_recv()
        settle(q, False)

    senders(take_grads, 1, lot_1)

    def take_r3(q):
        to_shard(r3.at[piece_at(q)], r3.at[piece_at(q)], r3_ss, r3_rs, q, q).wait_recv()

    peers(take_r3)
    whole = r3.at[pl.ds(0, width)]

    def send_r4(c):
        to_blk(whole, r4_in.at[mb], r4_ss, r4_rs, c, mb).start()

    blk_peers(send_r4)
    r4_in[mb] = r3[0:width]

    senders(take_grads, lot_1, n)

    def take_back(c):
        to_blk(back_out.at[c], back_in.at[c], back_ss, back_rs, c, c).wait_recv()
        own_back[...] += back_in[c].astype(F32)

    blk_peers(take_back)
    for h in range(own_rows // negatives):
        entity[:, h * negatives:(h + 1) * negatives] += jnp.where(sid == h, own_back[...], 0.0)

    def take_r4(c):
        to_blk(whole, r4_in.at[c], r4_ss, r4_rs, c, c).wait_recv()

    blk_peers(take_r4)
    for c in range(nb):
        wide = min(part, types - c * part)
        if wide > 0:
            relation_out[:, c * part:c * part + wide] = r4_in[c][:, 0:wide]

    def finish(q):
        to_shard(req_out.at[q], req_in.at[me], req_ss, req_rs, q, me).wait_send()
        to_shard(grad_out.at[q], grad_in.at[me], grad_ss, grad_rs, q, me).wait_send()
        to_shard(r2_out.at[piece_at(q)], r2_in.at[me], r2_ss, r2_rs, q, me).wait_send()
        to_shard(r3.at[piece_at(me)], r3.at[piece_at(me)], r3_ss, r3_rs, q, me).wait_send()

    peers(finish)

    def finish_blk(c):
        to_blk(spans.at[mb], spans.at[mb], span_ss, span_rs, c, mb).wait_send()
        to_blk(back_out.at[c], back_in.at[mb], back_ss, back_rs, c, mb).wait_send()
        to_blk(r1_out.at[c], r1_in.at[mb], r1_ss, r1_rs, c, mb).wait_send()
        to_blk(whole, r4_in.at[mb], r4_ss, r4_rs, c, mb).wait_send()

    blk_peers(finish_blk)


def round_up(a, b):
    return -(-a // b) * b


def shards(table, relation, owners, rows, rel_ids, span_ids):
    n = lax.axis_size("shard")
    nb = lax.axis_size("blk")
    edges = owners.shape[0]
    own_rows, width = table.shape
    types = relation.shape[0]
    cap = 4 * edges // n
    part = round_up(-(-types // nb), 128)
    piece = round_up(-(-width // n), 16)
    flat_owner = owners.T.reshape(-1)
    flat_row = rows.T.reshape(-1)
    hot = (flat_owner[None, :] == jnp.arange(n, dtype=jnp.int32)[:, None]).astype(jnp.int32)
    ranking = jnp.sum(jnp.cumsum(hot, axis=1) * hot, axis=0) - 1
    slots = (flat_owner * cap + ranking).reshape(1, 2 * edges)
    wanted = jnp.concatenate(
        [(flat_row // 256)[None], (flat_row % 256)[None], jnp.zeros((14, 2 * edges), jnp.int32)]
    ).astype(BF)

    vm = pltpu.VMEM
    dma = pltpu.SemaphoreType.DMA
    scratch = [
        vm((n, 8, cap), F32), vm((n, 8, cap), F32),
        vm((n, width, cap), BF), vm((n, width, cap), BF), vm((n, width, cap), BF),
        vm((nb, width, NEG), BF), vm((nb, width, NEG), BF), vm((nb, width, NEG), BF),
        vm((width, NEG), F32),
        vm((width, nb * part), BF), vm((width, edges), F32),
        vm((width, edges), F32), vm((width, edges), BF), vm((width, edges), F32),
        vm((width, 2 * edges), BF), vm((width, edges), BF),
        vm((nb, width, part), F32), vm((nb, width, part), F32),
        vm((n * piece, part), BF), vm((n, piece, part), BF), vm((n * piece, part), F32),
        vm((nb, width, part), F32),
    ]
    scratch += [dma((n,))] * 6 + [dma((nb,))] * 6 + [dma((n,))] * 4 + [dma((nb,))] * 2
    spec = pl.BlockSpec(memory_space=pltpu.VMEM)
    entity, rel_grad = pl.pallas_call(
        functools.partial(kernel, n, nb, cap, piece),
        out_shape=(
            jax.ShapeDtypeStruct((width, own_rows), F32),
            jax.ShapeDtypeStruct((width, types), F32),
        ),
        in_specs=[spec] * 6,
        out_specs=(spec, spec),
        scratch_shapes=scratch,
        compiler_params=pltpu.CompilerParams(
            collective_id=0, has_side_effects=True, vmem_limit_bytes=60 * 1024 * 1024
        ),
    )(table.T, relation.T, slots, wanted, rel_ids.reshape(1, edges), span_ids.reshape(1, 1))
    return (entity.T, rel_grad.T)


def solution(mesh):
    in_specs = (
        P(("blk", "shard"), None),
        P(),
        P(("blk", "shard"), None),
        P(("blk", "shard"), None),
        P(("blk", "shard")),
        P(("blk", "shard")),
    )
    out_specs = (P(("blk", "shard"), None), P())
    return jax.shard_map(shards, mesh=mesh, in_specs=in_specs, out_specs=out_specs, check_vma=False)
```
